512 devices in a mesh: ctx: 64 (over z, x), head: 8 (over y, core).
Axes of the slice: x: 4, y: 4, z: 16, core: 2. Of those that a mesh axis runs over, the one named last changes fastest.
Arguments:
- queries: bfloat16 [32768, 8192], P(('ctx', 'head')), may hold values from -170 to 170
- keys: bfloat16 [32768, 1024], P(('ctx', 'head')), may hold values from -6 to 6
- values: bfloat16 [32768, 1024], P(('ctx', 'head')), may hold values from -6 to 6
- doc_ids: int32 [32768], replicated, may hold values from 0 to 31, never falling along the last dimension, each value on 1 to 2561 neighbouring positions
Outputs:
- attended: bfloat16 [32768, 8192], P(('ctx', 'head'))
The draws below stay inside these ranges and needn't reach their ends.
Inputs may be any that keep to these rules, and one draw needn't show every extreme that they name: `doc_ids`: documents are contiguous runs, each of 1 to 2561 tokens, one exactly 2561.
All inputs are finite; a program needn't handle non-finite values.
Results may differ from the reference program's by a relative error of at most 0.0037.
Values may be sent and summed in bfloat16 or wider, within the bound.
No kernel may reach another device: no remote copies, remote signals or barrier semaphores. Data moves between devices by JAX's collectives and lax.ppermute only.
A program may use at most 64 MiB of HBM per device.

```python
import math
import jax
import jax.numpy as jnp
import numpy as np
from jax import lax

HQ = 64
KVH = 8
HD = 128
REACH = 5
BLOCK = 512
TOKENS = 32768
DOCS = 32
DOC_MOST = 2561
N_CTX = 64


def key_parts(key):
    shape = (TOKENS, KVH * HD)
    base_keys = jax.random.truncated_normal(jax.random.fold_in(key, 11), -6.0, 6.0, shape, jnp.float32)
    return base_keys


def draw_keys(key, part):
    base_keys = key_parts(key)
    return base_keys.astype(jnp.bfloat16)


def draw_queries(key, part):
    fresh = jax.random.truncated_normal(jax.random.fold_in(key, 13), -6.0, 6.0, (TOKENS, HQ * HD), jnp.float32)
    return fresh.astype(jnp.bfloat16)


def block_scale(stream_key, shape, shards, least, high):
    gain = 1.0
    for dim, blocks in shards:
        heights = jax.random.uniform(jax.random.fold_in(jax.random.fold_in(stream_key, 6), dim), (blocks,), jnp.float32, least / len(shards), high / len(shards))
        gain = gain * jnp.repeat(jnp.exp(heights), shape[dim] // blocks).reshape((-1,) + (1,) * (len(shape) - 1 - dim))
    return gain


def length_profile(number_of, total, bound, lean):
    loads = [(1 << 20) // math.isqrt(standing ** lean) + 1 for standing in range(2, number_of + 1)]
    rest, holding = total - bound - (number_of - 1), [1] * (number_of - 1)
    while rest > 0:
        free = [i for i in range(number_of - 1) if holding[i] < bound]
        mass, left = sum([loads[i] for i in free]), rest
        for i in free:
            more = min(bound - holding[i], max(1, left * loads[i] // mass), rest)
            holding[i] = holding[i] + more
            rest = rest - more
    return np.array([bound] + holding)


def uneven(rng, count, total, bound, slope):
    if count == 2:
        one = jax.random.randint(rng, (), max(1, total - bound), min(bound, total - 1) + 1)
        return jnp.stack([one, total - one])
    sizes = jnp.asarray(length_profile(count, total, bound, slope), jnp.int32)
    couples = (count - 1) // 2
    donor, receiver = sizes[1:1 + 2 * couples:2], sizes[2:2 + 2 * couples:2]
    room = jnp.minimum(donor - 1, bound - receiver)
    moved = jax.random.randint(jax.random.fold_in(rng, 1), (couples,), 0, 1 << 20) % (room + 1)
    sizes = sizes.at[1:1 + 2 * couples:2].set(donor - moved).at[2:2 + 2 * couples:2].set(receiver + moved)
    return sizes[jax.random.permutation(jax.random.fold_in(rng, 2), count)]


def bell_draw(own_key, shape, deviation, reach, shards=(), held_as=jnp.bfloat16):
    array = deviation * jax.random.normal(own_key, shape, jnp.float32)
    if shards:
        array = array * block_scale(own_key, shape, shards, -0.22, 0.18)
    return jnp.clip(array, -reach, reach).astype(held_as)


def setup_inputs(seed: int = 0) -> dict:
    key_list = jax.random.split(jax.random.key(seed), 5)
    queries = draw_queries(jax.random.fold_in(key_list[4], 71), 0)
    keys = draw_keys(jax.random.fold_in(key_list[4], 71), 0)
    values = bell_draw(key_list[2], (TOKENS, KVH * HD), 1.0, 6.0, ((0, 512),))
    doc_ids = jnp.searchsorted(jnp.cumsum(uneven(key_list[3], DOCS, TOKENS, DOC_MOST, 2)), jnp.arange(TOKENS), side="right").astype(jnp.int32)
    return {"queries": queries, "keys": keys, "values": values, "doc_ids": doc_ids}


def reference(queries, keys, values, doc_ids):
    window_len = (REACH + 1) * BLOCK
    group_size = HQ // KVH
    scaling = 1.0 / math.sqrt(HD)
    key_pad = jnp.concatenate([jnp.zeros((REACH * BLOCK, KVH * HD), jnp.bfloat16), keys], axis=0)
    value_pad = jnp.concatenate([jnp.zeros((REACH * BLOCK, KVH * HD), jnp.bfloat16), values], axis=0)
    doc_pad = jnp.concatenate([jnp.full((REACH * BLOCK,), -1, jnp.int32), doc_ids.astype(jnp.int32)])

    def one_block(block_number):
        first_row = (block_number * BLOCK).astype(jnp.int32)
        query_block = lax.dynamic_slice_in_dim(queries, first_row, BLOCK, 0).astype(jnp.float32)
        query_block = query_block.reshape(BLOCK, KVH, group_size, HD)
        key_block = lax.dynamic_slice_in_dim(key_pad, first_row, window_len, 0).astype(jnp.float32).reshape(window_len, KVH, HD)
        value_block = lax.dynamic_slice_in_dim(value_pad, first_row, window_len, 0).astype(jnp.float32).reshape(window_len, KVH, HD)
        query_docs = lax.dynamic_slice_in_dim(doc_ids.astype(jnp.int32), first_row, BLOCK, 0)
        key_docs = lax.dynamic_slice_in_dim(doc_pad, first_row, window_len, 0)
        query_pos = first_row + jnp.arange(BLOCK, dtype=jnp.int32)
        key_pos = first_row - REACH * BLOCK + jnp.arange(window_len, dtype=jnp.int32)
        visible = (query_docs[:, None] == key_docs[None, :]) & (key_pos[None, :] <= query_pos[:, None]) & (key_pos[None, :] >= 0)
        scores = jnp.einsum('qhgd,khd->hgqk', query_block, key_block) * scaling
        scores = jnp.where(visible[None, None], scores, -jnp.inf)
        peak = lax.optimization_barrier(jnp.max(scores, axis=-1, keepdims=True))
        weights = jnp.exp(scores - peak)
        totals = lax.optimization_barrier(jnp.sum(weights, axis=-1, keepdims=True))
        rounded = lax.optimization_barrier(weights.astype(jnp.bfloat16)).astype(jnp.float32)
        mixed = jnp.einsum('hgqk,khd->hgqd', rounded, value_block) / totals
        return jnp.transpose(mixed, (2, 0, 1, 3)).reshape(BLOCK, HQ * HD).astype(jnp.bfloat16)
    stacked = lax.map(one_block, jnp.arange(N_CTX, dtype=jnp.int32))
    return stacked.reshape(TOKENS, HQ * HD)
```

```python
import math

import jax
import jax.numpy as jnp
from jax import lax
from jax.experimental import pallas as pl
from jax.experimental.pallas import tpu as pltpu
from jax.sharding import Mesh
from jax.sharding import PartitionSpec as P

HD = 128
GRAN = 256
BACK = 10
OWN = 8
HALF = GRAN // 2
HEADS = 2
AXES = ("z", "x", "y", "core")
FACTOR = math.log2(math.e) / math.sqrt(HD)
HIDDEN = -2.0e30


def kernel(
    plan, q_ref, seen_ref, qdoc_ref, own_m, own_o, prev_m, prev_o, tail_m, tail_o,
    o_ref, ks, vs, acc, peak, sems,
):
    tile = pl.program_id(0)

    @pl.when(tile == 0)
    def _():
        copies = []
        number = 0
        for first, count, pair in (
            (BACK, OWN, (own_m, own_o)),
            (BACK - OWN, OWN, (prev_m, prev_o)),
            (0, BACK - OWN, (tail_m, tail_o)),
        ):
            for half, src in enumerate(pair):
                there = (pl.ds(first, count), pl.ds(half * HALF, HALF))
                for part, dst in ((0, ks), (1, vs)):
                    copy = pltpu.make_async_copy(
                        src.at[:, :, pl.ds(part * HD, HD)],
                        dst.at[there[0], there[1], pl.ds(0, HD)],
                        sems.at[number],
                    )
                    copy.start()
                    copies.append(copy)
                    number += 1
        vs[:, :, HD:] = jnp.ones((BACK + OWN, GRAN, HD), jnp.bfloat16)
        for copy in copies:
            copy.wait()

    diagonal = BACK + tile
    low = plan[0, tile]
    full = plan[1, tile]

    def step(first, count, masked, fresh):
        keys = ks[pl.ds(first, count)].reshape(count * GRAN, HD)
        values = vs[pl.ds(first, count)].reshape(count * GRAN, 2 * HD)
        if masked:
            kdoc = jnp.concatenate([seen_ref[first + k, 0:1] for k in range(count)], axis=1)
            kpos = jnp.concatenate([seen_ref[first + k, 1:2] for k in range(count)], axis=1)
            qdoc = jnp.concatenate([qdoc_ref[...]] * (count * 2), axis=1)
            qpos = diagonal * GRAN + lax.broadcasted_iota(jnp.int32, (GRAN, count * GRAN), 0)
            visible = (qdoc == kdoc) & (kpos <= qpos)
        for head in range(HEADS):
            query = q_ref[:, head * HD:(head + 1) * HD]
            scores = lax.dot_general(
                query, keys, (((1,), (1,)), ((), ())), preferred_element_type=jnp.float32
            )
            if masked:
                scores = jnp.where(visible, scores, HIDDEN)
            top = jnp.max(scores, axis=1, keepdims=True)
            if not fresh:
                before = peak[head]
                top = jnp.maximum(before[:, :1], top)
            weights = jnp.exp2((scores - top) * FACTOR).astype(jnp.bfloat16)
            mixed = jnp.dot(weights, values, preferred_element_type=jnp.float32)
            if fresh:
                acc[head] = mixed
            else:
                shrink = jnp.exp2((before[:, :1] - top) * FACTOR)
                acc[head] = acc[head] * shrink + mixed
            peak[head] = jnp.broadcast_to(top, (GRAN, HD))

    step(diagonal, 1, True, True)
    ahead = diagonal - low
    odd = lax.rem(ahead, 2)

    @pl.when(odd == 1)
    def _():
        step(low, 1, True, False)

    def pairs(number, carry):
        first = low + odd + 2 * number

        @pl.when(first < full)
        def _():
            step(first, 2, True, False)

        @pl.when(first >= full)
        def _():
            step(first, 2, False, False)

        return carry

    lax.fori_loop(0, lax.div(ahead, 2), pairs, 0)
    for head in range(HEADS):
        whole = acc[head]
        o_ref[:, head * HD:(head + 1) * HD] = (whole[:, :HD] / whole[:, HD:]).astype(jnp.bfloat16)


def attend(plan, queries, seen, qdoc, pieces):
    window = BACK + OWN
    rows = OWN * GRAN
    return pl.pallas_call(
        kernel,
        grid_spec=pltpu.PrefetchScalarGridSpec(
            num_scalar_prefetch=1,
            grid=(OWN,),
            in_specs=[
                pl.BlockSpec((GRAN, HEADS * HD), lambda i, plan: (i, 0)),
                pl.BlockSpec((window, 2, GRAN), lambda i, plan: (0, 0, 0)),
                pl.BlockSpec((GRAN, HD), lambda i, plan: (i, 0)),
            ]
            + [pl.BlockSpec(memory_space=pl.ANY)] * 6,
            out_specs=pl.BlockSpec((GRAN, HEADS * HD), lambda i, plan: (i, 0)),
            scratch_shapes=[
                pltpu.VMEM((window, GRAN, HD), jnp.bfloat16),
                pltpu.VMEM((window, GRAN, 2 * HD), jnp.bfloat16),
                pltpu.VMEM((HEADS, GRAN, 2 * HD), jnp.float32),
                pltpu.VMEM((HEADS, GRAN, HD), jnp.float32),
                pltpu.SemaphoreType.DMA((12,)),
            ],
        ),
        out_shape=jax.ShapeDtypeStruct((rows, HEADS * HD), jnp.bfloat16),
        compiler_params=pltpu.CompilerParams(vmem_limit_bytes=24 * 1024 * 1024),
        cost_estimate=pl.CostEstimate(
            flops=4 * rows * HEADS * HD * 1536,
            bytes_accessed=6 * 1024 * 1024,
            transcendentals=rows * HEADS * 1536,
        ),
    )(plan, queries, seen, qdoc, *pieces)


def moved(value, sizes, there):
    zs, xs, ys, cores = sizes
    pairs = []
    for z in range(zs):
        for x in range(xs):
            for y in range(ys):
                for core in range(cores):
                    place = there(z, x, y, core)
                    if place is not None:
                        index = [((p[0] * xs + p[1]) * ys + p[2]) * cores + p[3] for p in ((z, x, y, core), place)]
                        pairs.append(tuple(index))
    return lax.ppermute(value, AXES, pairs)


def body(sizes, queries, keys, values, doc_ids):
    zs, xs, ys, cores = sizes
    chips = xs * ys
    teams = chips * cores
    tokens = queries.shape[0]
    key_heads = keys.shape[1] // HD
    plane = OWN * GRAN
    swap = lambda z, x, y, core: (z, x, y, 1 - core)

    both = jnp.stack([keys.reshape(tokens, key_heads, HD), values.reshape(tokens, key_heads, HD)], axis=2)
    both = jnp.transpose(both.reshape(tokens, key_heads, 2 * HD), (1, 0, 2))
    both = jnp.repeat(both, chips // key_heads, axis=0)
    own_m = lax.all_to_all(both, ("x", "y"), 0, 0, tiled=True).reshape(OWN, HALF, 2 * HD)
    prev_m = moved(own_m, sizes, lambda z, x, y, core: (z + 1, x, y, core) if z + 1 < zs else None)
    tail_m = moved(own_m[2 * OWN - BACK:], sizes, lambda z, x, y, core: (z + 2, x, y, core) if z + 2 < zs else None)
    own_o = moved(own_m, sizes, swap)
    prev_o = moved(prev_m, sizes, swap)
    tail_o = moved(tail_m, sizes, swap)

    wide = jnp.transpose(queries.reshape(tokens, teams, HEADS * HD), (1, 0, 2))
    local = lax.all_to_all(wide, ("x", "y", "core"), 0, 0, tiled=True).reshape(plane, HEADS * HD)

    first = lax.axis_index("z") * plane
    padded = jnp.concatenate([jnp.full((BACK * GRAN,), -1, jnp.int32), doc_ids])
    window = lax.dynamic_slice_in_dim(padded, first, (BACK + OWN) * GRAN, 0)
    place = jnp.arange((BACK + OWN) * GRAN, dtype=jnp.int32)
    qids = window[BACK * GRAN:]
    starts = jnp.sum(
        window[None, None, :] < jnp.stack([qids[::GRAN], qids[GRAN - 1::GRAN]])[:, :, None],
        axis=2, dtype=jnp.int32,
    )
    plan = jnp.stack([starts[0] // GRAN, (starts[1] + GRAN - 1) // GRAN])
    core = lax.axis_index("core")

    def by_holder(line):
        split = jnp.transpose(line.reshape(BACK + OWN, GRAN // (cores * tokens), cores, tokens), (0, 2, 1, 3))
        split = split.reshape(BACK + OWN, cores, HALF)
        return jnp.where(core == 0, split, split[:, ::-1]).reshape(BACK + OWN, GRAN)

    seen = jnp.stack([by_holder(window), by_holder(place)], axis=1)
    qdoc = jnp.broadcast_to(qids[:, None], (plane, HD))

    out = attend(plan, local, seen, qdoc, (own_m, own_o, prev_m, prev_o, tail_m, tail_o))
    back = lax.all_to_all(out.reshape(teams, tokens, HEADS * HD), ("x", "y", "core"), 0, 0, tiled=True)
    return jnp.transpose(back, (1, 0, 2)).reshape(tokens, teams * HEADS * HD)


def solution(mesh):
    sizes = (16, 4, 4, 2)
    grid = Mesh(mesh.devices.reshape(sizes), AXES)

    def run(*args):
        return body(sizes, *args)

    return jax.shard_map(
        run,
        mesh=grid,
        in_specs=(P(AXES, None), P(AXES, None), P(AXES, None), P()),
        out_specs=P(AXES, None),
        check_vma=False,
    )
```

```python
import math

import jax
import jax.numpy as jnp
from jax import lax
from jax.experimental import pallas as pl
from jax.experimental.pallas import tpu as pltpu
from jax.sharding import Mesh
from jax.sharding import PartitionSpec as P

HD = 128
GRAN = 256
BACK = 10
OWN = 8
SPAN = 4
PAD = SPAN - 1
HALF = GRAN // 2
CHUNK = 64
HEADS = 2
COLS = HEADS * GRAN
ONES = 16
AXES = ("z", "x", "y", "core")
FACTOR = math.log2(math.e) / math.sqrt(HD)
HIDDEN = -2.0e30
FAR = 1 << 20
VMEM = pltpu.VMEM


def work(items, info, starts_ref, causal, ks, vt, qt, spot, acc, peak, sa, sb):
    def scored(number, buffer):
        tile, first = items[0, number], items[1, number]
        keys = ks[pl.ds(first, SPAN)].reshape(SPAN * GRAN, 2 * HD)
        raw = jnp.dot(keys, qt[tile], preferred_element_type=jnp.float32)
        low = starts_ref[tile] - (first - PAD) * GRAN + items[2, number]
        place = jnp.concatenate([spot[...]] * (COLS // HD), axis=1)
        best = None
        for k in range(SPAN):
            rows = slice(k * GRAN, (k + 1) * GRAN)
            seen = place >= jnp.concatenate([low - k * GRAN] * HEADS, axis=1)
            if causal and k == SPAN - 1:
                own = (tile - first) * GRAN + lax.broadcasted_iota(jnp.int32, (1, GRAN), 1)
                seen = seen & (place <= jnp.concatenate([own] * HEADS, axis=1))
            piece = jnp.where(seen, raw[rows], HIDDEN)
            buffer[rows] = piece
            most = jnp.max(piece.reshape(GRAN // 8, 8, COLS), axis=0)
            best = most if best is None else jnp.maximum(best, most)
        return jnp.max(best, axis=0, keepdims=True)

    def finish(number, buffer, best):
        tile, first = items[0, number], items[1, number]
        before = peak[tile]
        top = jnp.maximum(before, best)
        peak[tile] = top
        weights = jnp.exp2(buffer[...] - top).astype(jnp.bfloat16)
        values = vt[:, pl.ds(pl.multiple_of(first * GRAN, GRAN), SPAN * GRAN)]
        mixed = jnp.dot(values, weights, preferred_element_type=jnp.float32)
        acc[tile] = acc[tile] * jnp.exp2(before - top) + mixed

    def both(pair, best):
        following = scored(2 * pair + 1, sb)
        finish(2 * pair, sa, best)
        best = scored(2 * pair + 2, sa)
        finish(2 * pair + 1, sb, following)
        return best

    lax.fori_loop(0, info[0], both, scored(0, sa))


def fill(info, groups, ks, vt, stage, spot, sems):
    copies = []
    for first, count, pair in groups:
        for half, source in enumerate(pair):
            rows = pl.ds(half * HALF, HALF)
            for part, there in (
                (0, ks.at[pl.ds(PAD + first, count), rows, pl.ds(0, HD)]),
                (0, ks.at[pl.ds(PAD + first, count), rows, pl.ds(HD, HD)]),
                (1, stage.at[pl.ds(first, count), rows, :]),
            ):
                copy = pltpu.make_async_copy(
                    source.at[:, :, pl.ds(part * HD, HD)], there, sems.at[len(copies)]
                )
                copy.start()
                copies.append(copy)
    granules = stage.shape[0]
    ks[:PAD] = jnp.zeros((PAD, GRAN, 2 * HD), jnp.bfloat16)
    vt[:, :PAD * GRAN] = jnp.zeros((HD + ONES, PAD * GRAN), jnp.bfloat16)
    vt[HD:, PAD * GRAN:] = jnp.ones((ONES, granules * GRAN), jnp.bfloat16)
    row = lax.broadcasted_iota(jnp.int32, (GRAN, HD), 0)
    holder = jnp.where(info[1] == 0, row // HALF, 1 - row // HALF)
    inner = row % HALF
    spot[...] = (inner // CHUNK) * (2 * CHUNK) + holder * CHUNK + inner % CHUNK
    return copies


def turn(granules, vt, stage):
    for g in range(granules):
        vt[:HD, (PAD + g) * GRAN:(PAD + g + 1) * GRAN] = stage[g].T


def own_kernel(items, info, q_ref, starts_ref, own_m, own_o, qt, acc, peak, ks, vt, stage, spot, sa, sb, sems):
    copies = fill(info, ((0, OWN, (own_m, own_o)),), ks, vt, stage, spot, sems)
    acc[...] = jnp.zeros_like(acc)
    peak[...] = jnp.full_like(peak, HIDDEN)
    for tile in range(OWN):
        for head in range(HEADS):
            cols = slice(head * GRAN, (head + 1) * GRAN)
            query = q_ref[tile * GRAN:(tile + 1) * GRAN, head * HD:(head + 1) * HD].T.astype(jnp.float32) * FACTOR
            coarse = query.astype(jnp.bfloat16)
            qt[tile, :HD, cols] = coarse
            qt[tile, HD:, cols] = (query - coarse.astype(jnp.float32)).astype(jnp.bfloat16)
    for copy in copies:
        copy.wait()
    turn(OWN, vt, stage)
    work(items, info, starts_ref, True, ks, vt, qt, spot, acc, peak, sa, sb)


def back_kernel(
    items, info, starts_ref, qt, acc_in, peak_in, prev_m, prev_o, tail_m, tail_o,
    o_ref, acc, peak, ks, vt, stage, spot, sa, sb, sems,
):
    tail = BACK - OWN
    copies = fill(info, ((tail, OWN, (prev_m, prev_o)), (0, tail, (tail_m, tail_o))), ks, vt, stage, spot, sems)
    acc[...] = acc_in[...]
    peak[...] = peak_in[...]
    for copy in copies:
        copy.wait()
    turn(BACK, vt, stage)
    work(items, info, starts_ref, False, ks, vt, qt, spot, acc, peak, sa, sb)
    for tile in range(OWN):
        for head in range(HEADS):
            cols = slice(head * GRAN, (head + 1) * GRAN)
            o_ref[tile * GRAN:(tile + 1) * GRAN, head * HD:(head + 1) * HD] = (
                (acc[tile, :HD, cols] / acc[tile, HD:HD + 1, cols]).T.astype(jnp.bfloat16)
            )


def scratch(granules, copies):
    return [
        VMEM((PAD + granules, GRAN, 2 * HD), jnp.bfloat16),
        VMEM((HD + ONES, (PAD + granules) * GRAN), jnp.bfloat16),
        VMEM((granules, GRAN, HD), jnp.bfloat16),
        VMEM((GRAN, HD), jnp.int32),
        VMEM((SPAN * GRAN, COLS), jnp.float32),
        VMEM((SPAN * GRAN, COLS), jnp.float32),
        pltpu.SemaphoreType.DMA((copies,)),
    ]


STATE = ((OWN, HD + ONES, COLS), jnp.float32), ((OWN, 1, COLS), jnp.float32)
LIMIT = pltpu.CompilerParams(vmem_limit_bytes=40 * 1024 * 1024)
INSIDE = pl.BlockSpec(memory_space=VMEM)
ANYWHERE = pl.BlockSpec(memory_space=pl.ANY)


def attend_own(items, info, queries, starts, pair):
    shapes = (((OWN, 2 * HD, COLS), jnp.bfloat16),) + STATE
    return pl.pallas_call(
        own_kernel,
        grid_spec=pltpu.PrefetchScalarGridSpec(
            num_scalar_prefetch=2,
            grid=(),
            in_specs=[INSIDE, INSIDE, ANYWHERE, ANYWHERE],
            out_specs=[INSIDE] * 3,
            scratch_shapes=scratch(OWN, 6),
        ),
        out_shape=[jax.ShapeDtypeStruct(*s) for s in shapes],
        compiler_params=LIMIT,
        cost_estimate=pl.CostEstimate(flops=10**6, bytes_accessed=8 << 20, transcendentals=0),
    )(items, info, queries, starts, *pair)


def attend_back(items, info, starts, state, pieces):
    return pl.pallas_call(
        back_kernel,
        grid_spec=pltpu.PrefetchScalarGridSpec(
            num_scalar_prefetch=2,
            grid=(),
            in_specs=[INSIDE] * 4 + [ANYWHERE] * 4,
            out_specs=INSIDE,
            scratch_shapes=[VMEM(*s) for s in STATE] + scratch(BACK, 12),
        ),
        out_shape=jax.ShapeDtypeStruct((OWN * GRAN, HEADS * HD), jnp.bfloat16),
        compiler_params=LIMIT,
        cost_estimate=pl.CostEstimate(flops=8 * 10**9, bytes_accessed=8 << 20, transcendentals=0),
    )(items, info, starts, *state, *pieces)


def agenda(counts, tops, room, core):
    tiles = jnp.arange(OWN, dtype=jnp.int32)
    ends = jnp.sum(jnp.where(tiles[None, :] <= tiles[:, None], counts[None, :], 0), axis=1)
    number = jnp.arange(room, dtype=jnp.int32)
    tile = jnp.minimum(jnp.sum(number[:, None] >= ends[None, :], axis=1, dtype=jnp.int32), OWN - 1)
    real = number < ends[-1]
    chosen = tile[:, None] == tiles[None, :]
    begin = jnp.sum(jnp.where(chosen, (ends - counts)[None, :], 0), axis=1)
    top = jnp.sum(jnp.where(chosen, tops[None, :], 0), axis=1)
    first = top - SPAN * jnp.where(real, number - begin, 0)
    items = jnp.stack([tile, first, jnp.where(real, 0, FAR)])
    return items, jnp.stack([(ends[-1] + 1) // 2, core])


def plans(doc_ids, first, core):
    plane = OWN * GRAN
    padded = jnp.concatenate([jnp.full((BACK * GRAN,), -1, jnp.int32), doc_ids])
    window = lax.dynamic_slice_in_dim(padded, first, (BACK + OWN) * GRAN, 0)
    ids = window[BACK * GRAN:]
    starts = jnp.sum(window[None, :] < ids[:, None], axis=1, dtype=jnp.int32)
    lows = starts[::GRAN] // GRAN
    tiles = jnp.arange(OWN, dtype=jnp.int32)
    mine = agenda((tiles - jnp.maximum(lows - BACK, 0)) // SPAN + 1, tiles, 16, core)
    older = agenda((jnp.maximum(BACK - lows, 0) + SPAN - 1) // SPAN, jnp.full((OWN,), BACK - 1, jnp.int32), 32, core)
    starts = starts.reshape(OWN, 1, GRAN)
    return mine, older, jnp.maximum(starts - BACK * GRAN, 0), starts


def moved(value, sizes, there):
    zs, xs, ys, cores = sizes
    pairs = []
    for z in range(zs):
        for x in range(xs):
            for y in range(ys):
                for core in range(cores):
                    place = there(z, x, y, core)
                    if place is not None:
                        index = [((p[0] * xs + p[1]) * ys + p[2]) * cores + p[3] for p in ((z, x, y, core), place)]
                        pairs.append(tuple(index))
    return lax.ppermute(value, AXES, pairs)


def body(sizes, queries, keys, values, doc_ids):
    zs, xs, ys, cores = sizes
    chips = xs * ys
    teams = chips * cores
    tokens = queries.shape[0]
    key_heads = keys.shape[1] // HD
    plane = OWN * GRAN

    def swap(value):
        return moved(value, sizes, lambda z, x, y, core: (z, x, y, 1 - core))

    def later(value, planes):
        return moved(value, sizes, lambda z, x, y, core: (z + planes, x, y, core) if z + planes < zs else None)

    both = jnp.stack([keys.reshape(tokens, key_heads, HD), values.reshape(tokens, key_heads, HD)], axis=2)
    both = jnp.transpose(both.reshape(tokens, key_heads, 2 * HD), (1, 0, 2))
    both = jnp.repeat(both, chips // key_heads, axis=0)
    own_m = lax.all_to_all(both, ("x", "y"), 0, 0, tiled=True).reshape(OWN, HALF, 2 * HD)
    prev_m = later(own_m, 1)
    tail_m = later(own_m[2 * OWN - BACK:], 2)
    prev_m, tail_m = lax.optimization_barrier((prev_m, tail_m))
    own_o = swap(own_m)
    prev_o = swap(prev_m)
    tail_o = swap(tail_m)

    wide = jnp.transpose(queries.reshape(tokens, teams, HEADS * HD), (1, 0, 2))
    wide, _ = lax.optimization_barrier((wide, own_m))
    local = lax.all_to_all(wide, ("x", "y", "core"), 0, 0, tiled=True).reshape(plane, HEADS * HD)

    mine, older, near, far = plans(doc_ids, lax.axis_index("z") * plane, lax.axis_index("core"))
    state = attend_own(*mine, local, near, (own_m, own_o))
    out = attend_back(*older, far, state, (prev_m, prev_o, tail_m, tail_o))
    back = lax.all_to_all(out.reshape(teams, tokens, HEADS * HD), ("x", "y", "core"), 0, 0, tiled=True)
    return jnp.transpose(back, (1, 0, 2)).reshape(tokens, teams * HEADS * HD)


def solution(mesh):
    sizes = (16, 4, 4, 2)
    grid = Mesh(mesh.devices.reshape(sizes), AXES)

    def run(*args):
        return body(sizes, *args)

    return jax.shard_map(
        run,
        mesh=grid,
        in_specs=(P(AXES, None), P(AXES, None), P(AXES, None), P()),
        out_specs=P(AXES, None),
        check_vma=False,
    )
```

```python
import math

import jax
import jax.numpy as jnp
from jax import lax
from jax.experimental import pallas as pl
from jax.experimental.pallas import tpu as pltpu
from jax.sharding import Mesh
from jax.sharding import PartitionSpec as P

HD = 128
GRAN = 256
BACK = 10
OWN = 8
SPAN = 4
PAD = SPAN - 1
HALF = GRAN // 2
CHUNK = 64
HEADS = 2
COLS = HEADS * GRAN
ONES = 16
AXES = ("z", "x", "y", "core")
FACTOR = math.log2(math.e) / math.sqrt(HD)
HIDDEN = -2.0e30
FAR = 1 << 20
VMEM = pltpu.VMEM


def work(items, info, starts_ref, ks, vt, qt, spot, acc, peak, sa, sb):
    def scored(number, buffer):
        tile, first = items[0, number], items[1, number]
        keys = ks[pl.ds(first, SPAN)].reshape(SPAN * GRAN, 2 * HD)
        raw = jnp.dot(keys, qt[tile], preferred_element_type=jnp.float32)
        low = starts_ref[tile] - (first - PAD) * GRAN + items[2, number]
        place = jnp.concatenate([spot[...]] * (COLS // HD), axis=1)
        best = None
        for k in range(SPAN):
            rows = slice(k * GRAN, (k + 1) * GRAN)
            seen = place >= jnp.concatenate([low - k * GRAN] * HEADS, axis=1)
            if k == SPAN - 1:
                own = (BACK + tile - first) * GRAN + lax.broadcasted_iota(jnp.int32, (1, GRAN), 1)
                seen = seen & (place <= jnp.concatenate([own] * HEADS, axis=1))
            piece = jnp.where(seen, raw[rows], HIDDEN)
            buffer[rows] = piece
            most = jnp.max(piece.reshape(GRAN // 8, 8, COLS), axis=0)
            best = most if best is None else jnp.maximum(best, most)
        return jnp.max(best, axis=0, keepdims=True)

    def finish(number, buffer, best):
        tile, first = items[0, number], items[1, number]
        before = peak[tile]
        top = jnp.maximum(before, best)
        peak[tile] = top
        weights = jnp.exp2(buffer[...] - top).astype(jnp.bfloat16)
        values = vt[:, pl.ds(pl.multiple_of(first * GRAN, GRAN), SPAN * GRAN)]
        mixed = jnp.dot(values, weights, preferred_element_type=jnp.float32)
        acc[tile] = acc[tile] * jnp.exp2(before - top) + mixed

    def both(pair, best):
        following = scored(2 * pair + 1, sb)
        finish(2 * pair, sa, best)
        best = scored(2 * pair + 2, sa)
        finish(2 * pair + 1, sb, following)
        return best

    lax.fori_loop(0, info[0], both, scored(0, sa))


def fill(info, groups, ks, vt, stage, spot, sems):
    copies = []
    for first, count, pair in groups:
        for half, source in enumerate(pair):
            rows = pl.ds(half * HALF, HALF)
            for part, there in (
                (0, ks.at[pl.ds(PAD + first, count), rows, pl.ds(0, HD)]),
                (0, ks.at[pl.ds(PAD + first, count), rows, pl.ds(HD, HD)]),
                (1, stage.at[pl.ds(first, count), rows, :]),
            ):
                copy = pltpu.make_async_copy(
                    source.at[:, :, pl.ds(part * HD, HD)], there, sems.at[len(copies)]
                )
                copy.start()
                copies.append(copy)
    granules = stage.shape[0]
    ks[:PAD] = jnp.zeros((PAD, GRAN, 2 * HD), jnp.bfloat16)
    vt[:, :PAD * GRAN] = jnp.zeros((HD + ONES, PAD * GRAN), jnp.bfloat16)
    vt[HD:, PAD * GRAN:] = jnp.ones((ONES, granules * GRAN), jnp.bfloat16)
    row = lax.broadcasted_iota(jnp.int32, (GRAN, HD), 0)
    holder = jnp.where(info[1] == 0, row // HALF, 1 - row // HALF)
    inner = row % HALF
    spot[...] = (inner // CHUNK) * (2 * CHUNK) + holder * CHUNK + inner % CHUNK
    return copies


def turn(granules, vt, stage):
    for g in range(granules):
        vt[:HD, (PAD + g) * GRAN:(PAD + g + 1) * GRAN] = stage[g].T


def kernel(
    items, info, q_ref, starts_ref, own_m, own_o, prev_m, prev_o, tail_m, tail_o,
    o_ref, qt, acc, peak, ks, vt, stage, spot, sa, sb, sems,
):
    tail = BACK - OWN
    groups = (BACK, OWN, (own_m, own_o)), (tail, OWN, (prev_m, prev_o)), (0, tail, (tail_m, tail_o))
    copies = fill(info, groups, ks, vt, stage, spot, sems)
    acc[...] = jnp.zeros_like(acc)
    peak[...] = jnp.full_like(peak, HIDDEN)
    for tile in range(OWN):
        for head in range(HEADS):
            cols = slice(head * GRAN, (head + 1) * GRAN)
            query = q_ref[tile * GRAN:(tile + 1) * GRAN, head * HD:(head + 1) * HD].T.astype(jnp.float32) * FACTOR
            coarse = query.astype(jnp.bfloat16)
            qt[tile, :HD, cols] = coarse
            qt[tile, HD:, cols] = (query - coarse.astype(jnp.float32)).astype(jnp.bfloat16)
    for copy in copies:
        copy.wait()
    turn(BACK + OWN, vt, stage)
    work(items, info, starts_ref, ks, vt, qt, spot, acc, peak, sa, sb)
    for tile in range(OWN):
        for head in range(HEADS):
            cols = slice(head * GRAN, (head + 1) * GRAN)
            o_ref[tile * GRAN:(tile + 1) * GRAN, head * HD:(head + 1) * HD] = (
                (acc[tile, :HD, cols] / acc[tile, HD:HD + 1, cols]).T.astype(jnp.bfloat16)
            )


LIMIT = pltpu.CompilerParams(vmem_limit_bytes=40 * 1024 * 1024)
INSIDE = pl.BlockSpec(memory_space=VMEM)
ANYWHERE = pl.BlockSpec(memory_space=pl.ANY)


def attend(items, info, queries, starts, pieces):
    window = BACK + OWN
    return pl.pallas_call(
        kernel,
        grid_spec=pltpu.PrefetchScalarGridSpec(
            num_scalar_prefetch=2,
            grid=(),
            in_specs=[INSIDE] * 2 + [ANYWHERE] * 6,
            out_specs=INSIDE,
            scratch_shapes=[
                VMEM((OWN, 2 * HD, COLS), jnp.bfloat16),
                VMEM((OWN, HD + ONES, COLS), jnp.float32),
                VMEM((OWN, 1, COLS), jnp.float32),
                VMEM((PAD + window, GRAN, 2 * HD), jnp.bfloat16),
                VMEM((HD + ONES, (PAD + window) * GRAN), jnp.bfloat16),
                VMEM((window, GRAN, HD), jnp.bfloat16),
                VMEM((GRAN, HD), jnp.int32),
                VMEM((SPAN * GRAN, COLS), jnp.float32),
                VMEM((SPAN * GRAN, COLS), jnp.float32),
                pltpu.SemaphoreType.DMA((18,)),
            ],
        ),
        out_shape=jax.ShapeDtypeStruct((OWN * GRAN, HEADS * HD), jnp.bfloat16),
        compiler_params=LIMIT,
        cost_estimate=pl.CostEstimate(flops=10**10, bytes_accessed=8 << 20, transcendentals=0),
    )(items, info, queries, starts, *pieces)


def pack_kernel(k_ref, v_ref, o_ref):
    copies = o_ref.shape[0] * HD // k_ref.shape[1]
    for place in range(o_ref.shape[0]):
        cols = slice(place // copies * HD, (place // copies + 1) * HD)
        o_ref[place, :, :HD] = k_ref[:, cols]
        o_ref[place, :, HD:] = v_ref[:, cols]


def pack(keys, values, chips):
    return pl.pallas_call(
        pack_kernel,
        in_specs=[INSIDE] * 2,
        out_specs=INSIDE,
        out_shape=jax.ShapeDtypeStruct((chips, keys.shape[0], 2 * HD), jnp.bfloat16),
    )(keys, values)


def agenda(counts, tops, room, core):
    tiles = jnp.arange(OWN, dtype=jnp.int32)
    ends = jnp.sum(jnp.where(tiles[None, :] <= tiles[:, None], counts[None, :], 0), axis=1)
    number = jnp.arange(room, dtype=jnp.int32)
    tile = jnp.minimum(jnp.sum(number[:, None] >= ends[None, :], axis=1, dtype=jnp.int32), OWN - 1)
    real = number < ends[-1]
    chosen = tile[:, None] == tiles[None, :]
    begin = jnp.sum(jnp.where(chosen, (ends - counts)[None, :], 0), axis=1)
    top = jnp.sum(jnp.where(chosen, tops[None, :], 0), axis=1)
    first = top - SPAN * jnp.where(real, number - begin, 0)
    items = jnp.stack([tile, first, jnp.where(real, 0, FAR)])
    return items, jnp.stack([(ends[-1] + 1) // 2, core])


def plans(doc_ids, first, core):
    plane = OWN * GRAN
    padded = jnp.concatenate([jnp.full((BACK * GRAN,), -1, jnp.int32), doc_ids])
    window = lax.dynamic_slice_in_dim(padded, first, (BACK + OWN) * GRAN, 0)
    ids = window[BACK * GRAN:]
    starts = jnp.sum(window[None, :] < ids[:, None], axis=1, dtype=jnp.int32)
    lows = starts[::GRAN] // GRAN
    tiles = jnp.arange(OWN, dtype=jnp.int32)
    items, info = agenda((BACK + tiles - lows) // SPAN + 1, BACK + tiles, 32, core)
    return items, info, starts.reshape(OWN, 1, GRAN)


def moved(value, sizes, there):
    zs, xs, ys, cores = sizes
    pairs = []
    for z in range(zs):
        for x in range(xs):
            for y in range(ys):
                for core in range(cores):
                    place = there(z, x, y, core)
                    if place is not None:
                        index = [((p[0] * xs + p[1]) * ys + p[2]) * cores + p[3] for p in ((z, x, y, core), place)]
                        pairs.append(tuple(index))
    return lax.ppermute(value, AXES, pairs)


def body(sizes, queries, keys, values, doc_ids):
    zs, xs, ys, cores = sizes
    chips = xs * ys
    teams = chips * cores
    tokens = queries.shape[0]
    plane = OWN * GRAN

    def swap(value):
        return moved(value, sizes, lambda z, x, y, core: (z, x, y, 1 - core))

    def later(value, planes):
        return moved(value, sizes, lambda z, x, y, core: (z + planes, x, y, core) if z + planes < zs else None)

    own_m = lax.all_to_all(pack(keys, values, chips), ("x", "y"), 0, 0, tiled=True).reshape(OWN, HALF, 2 * HD)
    prev_m = later(own_m, 1)
    tail_m = later(own_m[2 * OWN - BACK:], 2)
    prev_m, tail_m = lax.optimization_barrier((prev_m, tail_m))
    own_o = swap(own_m)
    prev_o = swap(prev_m)
    tail_o = swap(tail_m)

    wide = jnp.transpose(queries.reshape(tokens, teams, HEADS * HD), (1, 0, 2))
    wide, _ = lax.optimization_barrier((wide, own_m))
    local = lax.all_to_all(wide, ("x", "y", "core"), 0, 0, tiled=True).reshape(plane, HEADS * HD)

    items, info, starts = plans(doc_ids, lax.axis_index("z") * plane, lax.axis_index("core"))
    out = attend(items, info, local, starts, (own_m, own_o, prev_m, prev_o, tail_m, tail_o))
    back = lax.all_to_all(out.reshape(teams, tokens, HEADS * HD), ("x", "y", "core"), 0, 0, tiled=True)
    return jnp.transpose(back, (1, 0, 2)).reshape(tokens, teams * HEADS * HD)


def solution(mesh):
    sizes = (16, 4, 4, 2)
    grid = Mesh(mesh.devices.reshape(sizes), AXES)

    def run(*args):
        return body(sizes, *args)

    return jax.shard_map(
        run,
        mesh=grid,
        in_specs=(P(AXES, None), P(AXES, None), P(AXES, None), P()),
        out_specs=P(AXES, None),
        check_vma=False,
    )
```

```python
import math

import jax
import jax.numpy as jnp
from jax import lax
from jax.experimental import pallas as pl
from jax.experimental.pallas import tpu as pltpu
from jax.sharding import Mesh
from jax.sharding import PartitionSpec as P

HD = 128
GRAN = 256
BACK = 10
OWN = 8
SPAN = 4
PAD = SPAN - 1
HALF = GRAN // 2
CHUNK = 64
HEADS = 2
COLS = HEADS * GRAN
ONES = 16
AXES = ("z", "x", "y", "core")
FACTOR = math.log2(math.e) / math.sqrt(HD)
HIDDEN = -2.0e30
FAR = 1 << 20
VMEM = pltpu.VMEM


def work(items, info, starts_ref, ks, vt, qt, spot, acc, peak, sa, sb):
    def scored(number, buffer):
        tile, first = items[0, number], items[1, number]
        keys = ks[pl.ds(first, SPAN)].reshape(SPAN * GRAN, 2 * HD)
        raw = jnp.dot(keys, qt[tile], preferred_element_type=jnp.float32)
        low = starts_ref[tile] - (first - PAD) * GRAN + items[2, number]
        place = jnp.concatenate([spot[...]] * (COLS // HD), axis=1)
        best = None
        for k in range(SPAN):
            rows = slice(k * GRAN, (k + 1) * GRAN)
            seen = place >= jnp.concatenate([low - k * GRAN] * HEADS, axis=1)
            if k == SPAN - 1:
                own = (BACK + tile - first) * GRAN + lax.broadcasted_iota(jnp.int32, (1, GRAN), 1)
                seen = seen & (place <= jnp.concatenate([own] * HEADS, axis=1))
            piece = jnp.where(seen, raw[rows], HIDDEN)
            buffer[rows] = piece
            most = jnp.max(piece.reshape(GRAN // 8, 8, COLS), axis=0)
            best = most if best is None else jnp.maximum(best, most)
        return jnp.max(best, axis=0, keepdims=True)

    def finish(number, buffer, best):
        tile, first = items[0, number], items[1, number]
        before = peak[tile]
        top = jnp.maximum(before, best)
        peak[tile] = top
        weights = jnp.exp2(buffer[...] - top).astype(jnp.bfloat16)
        values = vt[:, pl.ds(pl.multiple_of(first * GRAN, GRAN), SPAN * GRAN)]
        mixed = jnp.dot(values, weights, preferred_element_type=jnp.float32)
        acc[tile] = acc[tile] * jnp.exp2(before - top) + mixed

    def both(pair, best):
        following = scored(2 * pair + 1, sb)
        finish(2 * pair, sa, best)
        best = scored(2 * pair + 2, sa)
        finish(2 * pair + 1, sb, following)
        return best

    lax.fori_loop(0, info[0], both, scored(0, sa))


def fill(info, groups, ks, vt, stage, spot, sems):
    copies = []
    for first, count, pair in groups:
        for half, source in enumerate(pair):
            rows = pl.ds(half * HALF, HALF)
            for part, there in (
                (0, ks.at[pl.ds(PAD + first, count), rows, pl.ds(0, HD)]),
                (0, ks.at[pl.ds(PAD + first, count), rows, pl.ds(HD, HD)]),
                (1, stage.at[pl.ds(first, count), rows, :]),
            ):
                copy = pltpu.make_async_copy(
                    source.at[:, :, pl.ds(part * HD, HD)], there, sems.at[len(copies)]
                )
                copy.start()
                copies.append(copy)
    granules = stage.shape[0]
    ks[:PAD] = jnp.zeros((PAD, GRAN, 2 * HD), jnp.bfloat16)
    vt[:, :PAD * GRAN] = jnp.zeros((HD + ONES, PAD * GRAN), jnp.bfloat16)
    vt[HD:, PAD * GRAN:] = jnp.ones((ONES, granules * GRAN), jnp.bfloat16)
    row = lax.broadcasted_iota(jnp.int32, (GRAN, HD), 0)
    holder = jnp.where(info[1] == 0, row // HALF, 1 - row // HALF)
    inner = row % HALF
    spot[...] = (inner // CHUNK) * (2 * CHUNK) + holder * CHUNK + inner % CHUNK
    return copies


def turn(granules, vt, stage):
    for g in range(granules):
        vt[:HD, (PAD + g) * GRAN:(PAD + g + 1) * GRAN] = stage[g].T


def kernel(
    items, info, q_ref, starts_ref, own_m, own_o, prev_m, prev_o, tail_m, tail_o,
    o_ref, qt, acc, peak, ks, vt, stage, spot, sa, sb, sems,
):
    tail = BACK - OWN
    groups = (BACK, OWN, (own_m, own_o)), (tail, OWN, (prev_m, prev_o)), (0, tail, (tail_m, tail_o))
    copies = fill(info, groups, ks, vt, stage, spot, sems)
    acc[...] = jnp.zeros_like(acc)
    peak[...] = jnp.full_like(peak, HIDDEN)
    for tile in range(OWN):
        for head in range(HEADS):
            cols = slice(head * GRAN, (head + 1) * GRAN)
            query = q_ref[tile * GRAN:(tile + 1) * GRAN, head * HD:(head + 1) * HD].T.astype(jnp.float32) * FACTOR
            coarse = query.astype(jnp.bfloat16)
            qt[tile, :HD, cols] = coarse
            qt[tile, HD:, cols] = (query - coarse.astype(jnp.float32)).astype(jnp.bfloat16)
    for copy in copies:
        copy.wait()
    turn(BACK + OWN, vt, stage)
    work(items, info, starts_ref, ks, vt, qt, spot, acc, peak, sa, sb)
    for tile in range(OWN):
        for head in range(HEADS):
            cols = slice(head * GRAN, (head + 1) * GRAN)
            o_ref[tile * GRAN:(tile + 1) * GRAN, head * HD:(head + 1) * HD] = (
                (acc[tile, :HD, cols] / acc[tile, HD:HD + 1, cols]).T.astype(jnp.bfloat16)
            )


LIMIT = pltpu.CompilerParams(vmem_limit_bytes=40 * 1024 * 1024)
INSIDE = pl.BlockSpec(memory_space=VMEM)
ANYWHERE = pl.BlockSpec(memory_space=pl.ANY)


def attend(items, info, queries, starts, pieces):
    window = BACK + OWN
    return pl.pallas_call(
        kernel,
        grid_spec=pltpu.PrefetchScalarGridSpec(
            num_scalar_prefetch=2,
            grid=(),
            in_specs=[INSIDE] * 2 + [ANYWHERE] * 6,
            out_specs=INSIDE,
            scratch_shapes=[
                VMEM((OWN, 2 * HD, COLS), jnp.bfloat16),
                VMEM((OWN, HD + ONES, COLS), jnp.float32),
                VMEM((OWN, 1, COLS), jnp.float32),
                VMEM((PAD + window, GRAN, 2 * HD), jnp.bfloat16),
                VMEM((HD + ONES, (PAD + window) * GRAN), jnp.bfloat16),
                VMEM((window, GRAN, HD), jnp.bfloat16),
                VMEM((GRAN, HD), jnp.int32),
                VMEM((SPAN * GRAN, COLS), jnp.float32),
                VMEM((SPAN * GRAN, COLS), jnp.float32),
                pltpu.SemaphoreType.DMA((18,)),
            ],
        ),
        out_shape=jax.ShapeDtypeStruct((OWN * GRAN, HEADS * HD), jnp.bfloat16),
        compiler_params=LIMIT,
        cost_estimate=pl.CostEstimate(flops=10**10, bytes_accessed=8 << 20, transcendentals=0),
    )(items, info, queries, starts, *pieces)


def pack_kernel(k_ref, v_ref, o_ref):
    copies = o_ref.shape[0] * HD // k_ref.shape[1]
    for place in range(o_ref.shape[0]):
        cols = slice(place // copies * HD, (place // copies + 1) * HD)
        o_ref[place, :, :HD] = k_ref[:, cols]
        o_ref[place, :, HD:] = v_ref[:, cols]


def pack(keys, values, chips):
    return pl.pallas_call(
        pack_kernel,
        in_specs=[INSIDE] * 2,
        out_specs=INSIDE,
        out_shape=jax.ShapeDtypeStruct((chips, keys.shape[0], 2 * HD), jnp.bfloat16),
    )(keys, values)


def agenda(counts, tops, room, core):
    tiles = jnp.arange(OWN, dtype=jnp.int32)
    ends = jnp.sum(jnp.where(tiles[None, :] <= tiles[:, None], counts[None, :], 0), axis=1)
    number = jnp.arange(room, dtype=jnp.int32)
    tile = jnp.minimum(jnp.sum(number[:, None] >= ends[None, :], axis=1, dtype=jnp.int32), OWN - 1)
    real = number < ends[-1]
    chosen = tile[:, None] == tiles[None, :]
    begin = jnp.sum(jnp.where(chosen, (ends - counts)[None, :], 0), axis=1)
    top = jnp.sum(jnp.where(chosen, tops[None, :], 0), axis=1)
    first = top - SPAN * jnp.where(real, number - begin, 0)
    items = jnp.stack([tile, first, jnp.where(real, 0, FAR)])
    return items, jnp.stack([(ends[-1] + 1) // 2, core])


def plans(doc_ids, first, core):
    plane = OWN * GRAN
    padded = jnp.concatenate([jnp.full((BACK * GRAN,), -1, jnp.int32), doc_ids])
    window = lax.dynamic_slice_in_dim(padded, first, (BACK + OWN) * GRAN, 0)
    ids = window[BACK * GRAN:]
    starts = jnp.sum(window[None, :] < ids[:, None], axis=1, dtype=jnp.int32)
    lows = starts[::GRAN] // GRAN
    tiles = jnp.arange(OWN, dtype=jnp.int32)
    items, info = agenda((BACK + tiles - lows) // SPAN + 1, BACK + tiles, 32, core)
    return items, info, starts.reshape(OWN, 1, GRAN)


def moved(value, sizes, there):
    zs, xs, ys, cores = sizes
    pairs = []
    for z in range(zs):
        for x in range(xs):
            for y in range(ys):
                for core in range(cores):
                    place = there(z, x, y, core)
                    if place is not None:
                        index = [((p[0] * xs + p[1]) * ys + p[2]) * cores + p[3] for p in ((z, x, y, core), place)]
                        pairs.append(tuple(index))
    return lax.ppermute(value, AXES, pairs)


def body(sizes, queries, keys, values, doc_ids):
    zs, xs, ys, cores = sizes
    chips = xs * ys
    teams = chips * cores
    tokens = queries.shape[0]
    plane = OWN * GRAN

    def swap(value):
        return moved(value, sizes, lambda z, x, y, core: (z, x, y, 1 - core))

    def later(value, planes):
        return moved(value, sizes, lambda z, x, y, core: (z + planes, x, y, core) if z + planes < zs else None)

    own_m = lax.all_to_all(pack(keys, values, chips), ("x", "y"), 0, 0, tiled=True).reshape(OWN, HALF, 2 * HD)
    end = own_m[2 * OWN - BACK:]
    tail_m = later(end, 2)
    whole, _ = lax.optimization_barrier((own_m, end))
    prev_m = later(whole, 1)
    own_o = swap(own_m)
    tail_o = swap(tail_m)
    ready, _ = lax.optimization_barrier((prev_m, tail_o))
    prev_o = swap(ready)

    wide = jnp.transpose(queries.reshape(tokens, teams, HEADS * HD), (1, 0, 2))
    wide, _ = lax.optimization_barrier((wide, own_m))
    local = lax.all_to_all(wide, ("x", "y", "core"), 0, 0, tiled=True).reshape(plane, HEADS * HD)

    items, info, starts = plans(doc_ids, lax.axis_index("z") * plane, lax.axis_index("core"))
    out = attend(items, info, local, starts, (own_m, own_o, prev_m, prev_o, tail_m, tail_o))
    back = lax.all_to_all(out.reshape(teams, tokens, HEADS * HD), ("x", "y", "core"), 0, 0, tiled=True)
    return jnp.transpose(back, (1, 0, 2)).reshape(tokens, teams * HEADS * HD)


def solution(mesh):
    sizes = (16, 4, 4, 2)
    grid = Mesh(mesh.devices.reshape(sizes), AXES)

    def run(*args):
        return body(sizes, *args)

    return jax.shard_map(
        run,
        mesh=grid,
        in_specs=(P(AXES, None), P(AXES, None), P(AXES, None), P()),
        out_specs=P(AXES, None),
        check_vma=False,
    )
```

```python
import functools
import math

import jax
import jax.numpy as jnp
from jax import lax
from jax.experimental import pallas as pl
from jax.experimental.pallas import tpu as pltpu
from jax.sharding import Mesh
from jax.sharding import PartitionSpec as P

HD = 128
GRAN = 256
BACK = 10
OWN = 8
PARTS = 2
TILES = OWN // PARTS
SPAN = 4
PAD = SPAN - 1
HALF = GRAN // 2
CHUNK = 64
HEADS = 2
COLS = HEADS * GRAN
ONES = 16
AXES = ("z", "x", "y", "core")
FACTOR = math.log2(math.e) / math.sqrt(HD)
HIDDEN = -2.0e30
FAR = 1 << 20
VMEM = pltpu.VMEM


def work(part, items, info, starts_ref, ks, vt, qt, spot, acc, peak, sa, sb):
    piece = CHUNK // PARTS
    column = lax.broadcasted_iota(jnp.int32, (1, GRAN), 1)
    line = (column // piece) * CHUNK + part * piece + column % piece

    def scored(number, buffer):
        tile, first = items[0, number], items[1, number]
        keys = ks[pl.ds(first, SPAN)].reshape(SPAN * GRAN, 2 * HD)
        raw = jnp.dot(keys, qt[tile], preferred_element_type=jnp.float32)
        low = starts_ref[tile] - (first - PAD) * GRAN + items[2, number]
        upper = line + (BACK + PARTS * tile - (first - PAD)) * GRAN
        place = jnp.concatenate([spot[...]] * (COLS // HD), axis=1)
        best = None
        for k in range(SPAN):
            rows = slice(k * GRAN, (k + 1) * GRAN)
            seen = place >= jnp.concatenate([low - k * GRAN] * HEADS, axis=1)
            if k >= SPAN - PARTS:
                own = upper - k * GRAN
                seen = seen & (place <= jnp.concatenate([own] * HEADS, axis=1))
            piece = jnp.where(seen, raw[rows], HIDDEN)
            buffer[rows] = piece
            most = jnp.max(piece.reshape(GRAN // 8, 8, COLS), axis=0)
            best = most if best is None else jnp.maximum(best, most)
        return jnp.max(best, axis=0, keepdims=True)

    def finish(number, buffer, best):
        tile, first = items[0, number], items[1, number]
        before = peak[tile]
        top = jnp.maximum(before, best)
        peak[tile] = top
        weights = jnp.exp2(buffer[...] - top).astype(jnp.bfloat16)
        values = vt[:, pl.ds(pl.multiple_of(first * GRAN, GRAN), SPAN * GRAN)]
        mixed = jnp.dot(values, weights, preferred_element_type=jnp.float32)
        acc[tile] = acc[tile] * jnp.exp2(before - top) + mixed

    def both(pair, best):
        following = scored(2 * pair + 1, sb)
        finish(2 * pair, sa, best)
        best = scored(2 * pair + 2, sa)
        finish(2 * pair + 1, sb, following)
        return best

    lax.fori_loop(0, info[0], both, scored(0, sa))


def fill(groups, ks, vt, stage, sems):
    copies = []
    for first, half, source in groups:
        count, rows = source.shape[0], pl.ds(half * HALF, HALF)
        for part, there in (
            (0, ks.at[pl.ds(PAD + first, count), rows, pl.ds(0, HD)]),
            (0, ks.at[pl.ds(PAD + first, count), rows, pl.ds(HD, HD)]),
            (1, stage.at[pl.ds(first, count), rows, :]),
        ):
            copy = pltpu.make_async_copy(source.at[:, :, pl.ds(part * HD, HD)], there, sems.at[len(copies)])
            copy.start()
            copies.append(copy)
    granules = stage.shape[0]
    ks[:PAD] = jnp.zeros((PAD, GRAN, 2 * HD), jnp.bfloat16)
    vt[:, :PAD * GRAN] = jnp.zeros((HD + ONES, PAD * GRAN), jnp.bfloat16)
    vt[HD:, PAD * GRAN:] = jnp.ones((ONES, granules * GRAN), jnp.bfloat16)
    return copies


def places(info, spot):
    row = lax.broadcasted_iota(jnp.int32, (GRAN, HD), 0)
    holder = jnp.where(info[1] == 0, row // HALF, 1 - row // HALF)
    inner = row % HALF
    spot[...] = (inner // CHUNK) * (2 * CHUNK) + holder * CHUNK + inner % CHUNK


def turn(granules, vt, stage):
    for g in range(granules):
        vt[:HD, (PAD + g) * GRAN:(PAD + g + 1) * GRAN] = stage[g].T


def attention(part, items, info, q_ref, starts_ref, o_ref, ks, vt, ready, qt, acc, peak, spot, sa, sb):
    places(info, spot)
    acc[...] = jnp.zeros_like(acc)
    peak[...] = jnp.full_like(peak, HIDDEN)
    piece = CHUNK // PARTS
    devices = GRAN // piece
    for tile in range(TILES):
        rows = q_ref[tile * devices:(tile + 1) * devices, part * piece:(part + 1) * piece, :].reshape(GRAN, HEADS * HD)
        for head in range(HEADS):
            cols = slice(head * GRAN, (head + 1) * GRAN)
            query = rows[:, head * HD:(head + 1) * HD].T.astype(jnp.float32) * FACTOR
            coarse = query.astype(jnp.bfloat16)
            qt[tile, :HD, cols] = coarse
            qt[tile, HD:, cols] = (query - coarse.astype(jnp.float32)).astype(jnp.bfloat16)
    ready()
    work(part, items, info, starts_ref, ks, vt, qt, spot, acc, peak, sa, sb)
    for tile in range(TILES):
        for head in range(HEADS):
            cols = slice(head * GRAN, (head + 1) * GRAN)
            o_ref[tile * GRAN:(tile + 1) * GRAN, head * HD:(head + 1) * HD] = (
                (acc[tile, :HD, cols] / acc[tile, HD:HD + 1, cols]).T.astype(jnp.bfloat16)
            )


def kernel(
    part, items, info, q_ref, starts_ref, own_m, own_o, prev_m, tail_m, older_o,
    o_ref, ks, vt, stage, sems, *rest,
):
    tail = BACK - OWN
    groups = (BACK, 0, own_m), (BACK, 1, own_o), (tail, 0, prev_m), (0, 0, tail_m), (0, 1, older_o)
    copies = fill(groups, ks, vt, stage, sems)

    def ready():
        for copy in copies:
            copy.wait()
        turn(BACK + OWN, vt, stage)

    attention(part, items, info, q_ref, starts_ref, o_ref, ks, vt, ready, *rest)


LIMIT = pltpu.CompilerParams(vmem_limit_bytes=24 * 1024 * 1024)
INSIDE = pl.BlockSpec(memory_space=VMEM)
ANYWHERE = pl.BlockSpec(memory_space=pl.ANY)
WINDOW = BACK + OWN
RESULT = jax.ShapeDtypeStruct((TILES * GRAN, HEADS * HD), jnp.bfloat16)
SCRATCH = [
    VMEM((PAD + WINDOW, GRAN, 2 * HD), jnp.bfloat16),
    VMEM((HD + ONES, (PAD + WINDOW) * GRAN), jnp.bfloat16),
    VMEM((WINDOW, GRAN, HD), jnp.bfloat16),
    pltpu.SemaphoreType.DMA((15,)),
    VMEM((TILES, 2 * HD, COLS), jnp.bfloat16),
    VMEM((TILES, HD + ONES, COLS), jnp.float32),
    VMEM((TILES, 1, COLS), jnp.float32),
    VMEM((GRAN, HD), jnp.int32),
    VMEM((SPAN * GRAN, COLS), jnp.float32),
    VMEM((SPAN * GRAN, COLS), jnp.float32),
]
COST = pl.CostEstimate(flops=3 * 10**10, bytes_accessed=4 << 20, transcendentals=0)


def attend(part, items, info, starts, queries, pieces):
    return pl.pallas_call(
        functools.partial(kernel, part),
        grid_spec=pltpu.PrefetchScalarGridSpec(
            num_scalar_prefetch=2,
            grid=(),
            in_specs=[INSIDE] * 2 + [ANYWHERE] * 5,
            out_specs=INSIDE,
            scratch_shapes=SCRATCH,
        ),
        out_shape=RESULT,
        compiler_params=LIMIT,
        cost_estimate=COST,
    )(items, info, queries, starts, *pieces)


def pack_kernel(k_ref, v_ref, o_ref):
    copies = o_ref.shape[0] * HD // k_ref.shape[1]
    for place in range(o_ref.shape[0]):
        cols = slice(place // copies * HD, (place // copies + 1) * HD)
        o_ref[place, :, :HD] = k_ref[:, cols]
        o_ref[place, :, HD:] = v_ref[:, cols]


def pack(keys, values, chips):
    return pl.pallas_call(
        pack_kernel,
        in_specs=[INSIDE] * 2,
        out_specs=INSIDE,
        out_shape=jax.ShapeDtypeStruct((chips, keys.shape[0], 2 * HD), jnp.bfloat16),
    )(keys, values)


def agenda(starts, core, room):
    tiles = jnp.arange(TILES, dtype=jnp.int32)
    tops = BACK + PARTS * tiles + PARTS - 1
    counts = (tops - starts[:, 0] // GRAN) // SPAN + 1
    ends = jnp.sum(jnp.where(tiles[None, :] <= tiles[:, None], counts[None, :], 0), axis=1)
    number = jnp.arange(room, dtype=jnp.int32)
    tile = jnp.minimum(jnp.sum(number[:, None] >= ends[None, :], axis=1, dtype=jnp.int32), TILES - 1)
    real = number < ends[-1]
    chosen = tile[:, None] == tiles[None, :]
    begin = jnp.sum(jnp.where(chosen, (ends - counts)[None, :], 0), axis=1)
    top = jnp.sum(jnp.where(chosen, tops[None, :], 0), axis=1)
    first = top - SPAN * jnp.where(real, number - begin, 0)
    items = jnp.stack([tile, first, jnp.where(real, 0, FAR)])
    return items, jnp.stack([(ends[-1] + 1) // 2, core])


def plans(doc_ids, first, core):
    plane = OWN * GRAN
    padded = jnp.concatenate([jnp.full((BACK * GRAN,), -1, jnp.int32), doc_ids])
    window = lax.dynamic_slice_in_dim(padded, first, (BACK + OWN) * GRAN, 0)
    ids = window[BACK * GRAN:]
    starts = jnp.sum(window[None, :] < ids[:, None], axis=1, dtype=jnp.int32)
    starts = starts.reshape(plane // CHUNK, PARTS, CHUNK // PARTS)
    parts = [starts[:, part].reshape(TILES, GRAN) for part in range(PARTS)]
    return [agenda(part, core, 16) + (part.reshape(TILES, 1, GRAN),) for part in parts]


def moved(value, sizes, there):
    zs, xs, ys, cores = sizes
    pairs = []
    for z in range(zs):
        for x in range(xs):
            for y in range(ys):
                for core in range(cores):
                    place = there(z, x, y, core)
                    if place is not None:
                        index = [((p[0] * xs + p[1]) * ys + p[2]) * cores + p[3] for p in ((z, x, y, core), place)]
                        pairs.append(tuple(index))
    return lax.ppermute(value, AXES, pairs)


def body(sizes, queries, keys, values, doc_ids):
    zs, xs, ys, cores = sizes
    chips = xs * ys
    teams = chips * cores
    tokens = queries.shape[0]
    plane = OWN * GRAN

    def swap(value):
        return moved(value, sizes, lambda z, x, y, core: (z, x, y, 1 - core))

    def later(value, planes):
        return moved(value, sizes, lambda z, x, y, core: (z + planes, x, y, core) if z + planes < zs else None)

    own_m = lax.all_to_all(pack(keys, values, chips), ("x", "y"), 0, 0, tiled=True).reshape(OWN, HALF, 2 * HD)
    prev_m = later(own_m, 1)
    tail_m = later(own_m[2 * OWN - BACK:], 2)
    own_o = swap(own_m)
    older_o = swap(jnp.concatenate([tail_m, prev_m]))

    wide = jnp.transpose(queries.reshape(tokens, teams, HEADS * HD), (1, 0, 2))
    wide, _ = lax.optimization_barrier((wide, own_m))
    local = lax.all_to_all(wide, ("x", "y", "core"), 0, 0, tiled=True)

    def returned(out):
        back = lax.all_to_all(out.reshape(teams, tokens // PARTS, HEADS * HD), ("x", "y", "core"), 0, 0, tiled=True)
        return jnp.transpose(back, (1, 0, 2)).reshape(tokens // PARTS, teams * HEADS * HD)

    agendas = plans(doc_ids, lax.axis_index("z") * plane, lax.axis_index("core"))
    pieces = (own_m, own_o, prev_m, tail_m, older_o)
    outs = [attend(part, *agendas[part], local, pieces) for part in range(PARTS)]
    front = returned(outs[0])
    rest, front = lax.optimization_barrier((outs[1], front))
    return jnp.concatenate([front, returned(rest)], axis=0)


def solution(mesh):
    sizes = (16, 4, 4, 2)
    grid = Mesh(mesh.devices.reshape(sizes), AXES)

    def run(*args):
        return body(sizes, *args)

    return jax.shard_map(
        run,
        mesh=grid,
        in_specs=(P(AXES, None), P(AXES, None), P(AXES, None), P()),
        out_specs=P(AXES, None),
        check_vma=False,
    )
```

```python
import math

import jax
import jax.numpy as jnp
from jax import lax
from jax.experimental import pallas as pl
from jax.experimental.pallas import tpu as pltpu
from jax.sharding import Mesh
from jax.sharding import PartitionSpec as P

HD = 128
GRAN = 256
BACK = 10
OWN = 8
SPAN = 2
PAD = SPAN - 1
HALF = GRAN // 2
CHUNK = 64
HEADS = 2
COLS = HEADS * GRAN
ONES = 16
AXES = ("z", "x", "y", "core")
FACTOR = math.log2(math.e) / math.sqrt(HD)
HIDDEN = -2.0e30
FAR = 1 << 20
VMEM = pltpu.VMEM


def work(items, info, starts_ref, ks, vt, qt, spot, acc, peak, sa, sb):
    def scored(number, buffer):
        tile, first = items[0, number], items[1, number]
        keys = ks[pl.ds(first, SPAN)].reshape(SPAN * GRAN, 2 * HD)
        raw = jnp.dot(keys, qt[tile], preferred_element_type=jnp.float32)
        low = starts_ref[tile] - (first - PAD) * GRAN + items[2, number]
        place = jnp.concatenate([spot[...]] * (COLS // HD), axis=1)
        best = None
        for k in range(SPAN):
            rows = slice(k * GRAN, (k + 1) * GRAN)
            seen = place >= jnp.concatenate([low - k * GRAN] * HEADS, axis=1)
            if k == SPAN - 1:
                own = (BACK + tile - first) * GRAN + lax.broadcasted_iota(jnp.int32, (1, GRAN), 1)
                seen = seen & (place <= jnp.concatenate([own] * HEADS, axis=1))
            piece = jnp.where(seen, raw[rows], HIDDEN)
            buffer[rows] = piece
            most = jnp.max(piece.reshape(GRAN // 8, 8, COLS), axis=0)
            best = most if best is None else jnp.maximum(best, most)
        return jnp.max(best, axis=0, keepdims=True)

    def finish(number, buffer, best):
        tile, first = items[0, number], items[1, number]
        before = peak[tile]
        top = jnp.maximum(before, best)
        peak[tile] = top
        weights = jnp.exp2(buffer[...] - top).astype(jnp.bfloat16)
        values = vt[:, pl.ds(pl.multiple_of(first * GRAN, GRAN), SPAN * GRAN)]
        mixed = jnp.dot(values, weights, preferred_element_type=jnp.float32)
        acc[tile] = acc[tile] * jnp.exp2(before - top) + mixed

    def both(first, best):
        following = scored(first + 1, sb)
        finish(first, sa, best)
        best = scored(first + 2, sa)
        finish(first + 1, sb, following)
        return best

    def several(pairs, done, best):
        def group(number, best):
            for pair in range(pairs):
                best = both(2 * (done + pairs * number + pair), best)
            return best

        groups = lax.div(info[0] - done, pairs)
        return done + pairs * groups, lax.fori_loop(0, groups, group, best)

    done, best = 0, scored(0, sa)
    for pairs in (4, 2, 1):
        done, best = several(pairs, done, best)


def fill(info, groups, ks, vt, stage, spot, sems):
    copies = []
    for first, half, source in groups:
        count, rows = source.shape[0], pl.ds(half * HALF, HALF)
        for part, there in (
            (0, ks.at[pl.ds(PAD + first, count), rows, pl.ds(0, HD)]),
            (0, ks.at[pl.ds(PAD + first, count), rows, pl.ds(HD, HD)]),
            (1, stage.at[pl.ds(first, count), rows, :]),
        ):
            copy = pltpu.make_async_copy(source.at[:, :, pl.ds(part * HD, HD)], there, sems.at[len(copies)])
            copy.start()
            copies.append(copy)
    granules = stage.shape[0]
    ks[:PAD] = jnp.zeros((PAD, GRAN, 2 * HD), jnp.bfloat16)
    vt[:, :PAD * GRAN] = jnp.zeros((HD + ONES, PAD * GRAN), jnp.bfloat16)
    vt[HD:, PAD * GRAN:] = jnp.ones((ONES, granules * GRAN), jnp.bfloat16)
    row = lax.broadcasted_iota(jnp.int32, (GRAN, HD), 0)
    holder = jnp.where(info[1] == 0, row // HALF, 1 - row // HALF)
    inner = row % HALF
    spot[...] = (inner // CHUNK) * (2 * CHUNK) + holder * CHUNK + inner % CHUNK
    return copies


def turn(granules, vt, stage):
    for g in range(granules):
        vt[:HD, (PAD + g) * GRAN:(PAD + g + 1) * GRAN] = stage[g].T


def kernel(
    items, info, q_ref, starts_ref, own_m, own_o, prev_m, tail_m, older_o,
    o_ref, qt, acc, peak, ks, vt, stage, spot, sa, sb, sems,
):
    tail = BACK - OWN
    groups = (BACK, 0, own_m), (BACK, 1, own_o), (tail, 0, prev_m), (0, 0, tail_m), (0, 1, older_o)
    copies = fill(info, groups, ks, vt, stage, spot, sems)
    acc[...] = jnp.zeros_like(acc)
    peak[...] = jnp.full_like(peak, HIDDEN)
    for tile in range(OWN):
        for head in range(HEADS):
            cols = slice(head * GRAN, (head + 1) * GRAN)
            query = q_ref[tile * GRAN:(tile + 1) * GRAN, head * HD:(head + 1) * HD].T.astype(jnp.float32) * FACTOR
            coarse = query.astype(jnp.bfloat16)
            qt[tile, :HD, cols] = coarse
            qt[tile, HD:, cols] = (query - coarse.astype(jnp.float32)).astype(jnp.bfloat16)
    for copy in copies:
        copy.wait()
    turn(BACK + OWN, vt, stage)
    work(items, info, starts_ref, ks, vt, qt, spot, acc, peak, sa, sb)
    for tile in range(OWN):
        for head in range(HEADS):
            cols = slice(head * GRAN, (head + 1) * GRAN)
            o_ref[tile * GRAN:(tile + 1) * GRAN, head * HD:(head + 1) * HD] = (
                (acc[tile, :HD, cols] / acc[tile, HD:HD + 1, cols]).T.astype(jnp.bfloat16)
            )


LIMIT = pltpu.CompilerParams(vmem_limit_bytes=40 * 1024 * 1024)
INSIDE = pl.BlockSpec(memory_space=VMEM)
ANYWHERE = pl.BlockSpec(memory_space=pl.ANY)


def attend(items, info, queries, starts, pieces):
    window = BACK + OWN
    return pl.pallas_call(
        kernel,
        grid_spec=pltpu.PrefetchScalarGridSpec(
            num_scalar_prefetch=2,
            grid=(),
            in_specs=[INSIDE] * 2 + [ANYWHERE] * 5,
            out_specs=INSIDE,
            scratch_shapes=[
                VMEM((OWN, 2 * HD, COLS), jnp.bfloat16),
                VMEM((OWN, HD + ONES, COLS), jnp.float32),
                VMEM((OWN, 1, COLS), jnp.float32),
                VMEM((PAD + window, GRAN, 2 * HD), jnp.bfloat16),
                VMEM((HD + ONES, (PAD + window) * GRAN), jnp.bfloat16),
                VMEM((window, GRAN, HD), jnp.bfloat16),
                VMEM((GRAN, HD), jnp.int32),
                VMEM((SPAN * GRAN, COLS), jnp.float32),
                VMEM((SPAN * GRAN, COLS), jnp.float32),
                pltpu.SemaphoreType.DMA((15,)),
            ],
        ),
        out_shape=jax.ShapeDtypeStruct((OWN * GRAN, HEADS * HD), jnp.bfloat16),
        compiler_params=LIMIT,
        cost_estimate=pl.CostEstimate(flops=10**10, bytes_accessed=8 << 20, transcendentals=0),
    )(items, info, queries, starts, *pieces)


def pack_kernel(k_ref, v_ref, o_ref):
    copies = o_ref.shape[0] * HD // k_ref.shape[1]
    for place in range(o_ref.shape[0]):
        cols = slice(place // copies * HD, (place // copies + 1) * HD)
        o_ref[place, :, :HD] = k_ref[:, cols]
        o_ref[place, :, HD:] = v_ref[:, cols]


def pack(keys, values, chips):
    return pl.pallas_call(
        pack_kernel,
        in_specs=[INSIDE] * 2,
        out_specs=INSIDE,
        out_shape=jax.ShapeDtypeStruct((chips, keys.shape[0], 2 * HD), jnp.bfloat16),
    )(keys, values)


def agenda(counts, tops, room, core):
    tiles = jnp.arange(OWN, dtype=jnp.int32)
    ends = jnp.sum(jnp.where(tiles[None, :] <= tiles[:, None], counts[None, :], 0), axis=1)
    number = jnp.arange(room, dtype=jnp.int32)
    tile = jnp.minimum(jnp.sum(number[:, None] >= ends[None, :], axis=1, dtype=jnp.int32), OWN - 1)
    real = number < ends[-1]
    chosen = tile[:, None] == tiles[None, :]
    begin = jnp.sum(jnp.where(chosen, (ends - counts)[None, :], 0), axis=1)
    top = jnp.sum(jnp.where(chosen, tops[None, :], 0), axis=1)
    first = top - SPAN * jnp.where(real, number - begin, 0)
    items = jnp.stack([tile, first, jnp.where(real, 0, FAR)])
    return items, jnp.stack([(ends[-1] + 1) // 2, core])


def plans(doc_ids, first, core):
    plane = OWN * GRAN
    padded = jnp.concatenate([jnp.full((BACK * GRAN,), -1, jnp.int32), doc_ids])
    window = lax.dynamic_slice_in_dim(padded, first, (BACK + OWN) * GRAN, 0)
    ids = window[BACK * GRAN:]
    starts = jnp.sum(window[None, :] < ids[:, None], axis=1, dtype=jnp.int32)
    lows = starts[::GRAN] // GRAN
    tiles = jnp.arange(OWN, dtype=jnp.int32)
    items, info = agenda((BACK + tiles - lows) // SPAN + 1, BACK + tiles, 52, core)
    return items, info, starts.reshape(OWN, 1, GRAN)


def moved(value, sizes, there):
    zs, xs, ys, cores = sizes
    pairs = []
    for z in range(zs):
        for x in range(xs):
            for y in range(ys):
                for core in range(cores):
                    place = there(z, x, y, core)
                    if place is not None:
                        index = [((p[0] * xs + p[1]) * ys + p[2]) * cores + p[3] for p in ((z, x, y, core), place)]
                        pairs.append(tuple(index))
    return lax.ppermute(value, AXES, pairs)


def body(sizes, queries, keys, values, doc_ids):
    zs, xs, ys, cores = sizes
    chips = xs * ys
    teams = chips * cores
    tokens = queries.shape[0]
    plane = OWN * GRAN

    def swap(value):
        return moved(value, sizes, lambda z, x, y, core: (z, x, y, 1 - core))

    def later(value, planes):
        return moved(value, sizes, lambda z, x, y, core: (z + planes, x, y, core) if z + planes < zs else None)

    own_m = lax.all_to_all(pack(keys, values, chips), ("x", "y"), 0, 0, tiled=True).reshape(OWN, HALF, 2 * HD)
    prev_m = later(own_m, 1)
    tail_m = later(own_m[2 * OWN - BACK:], 2)
    own_o = swap(own_m)
    older_m, own_o = lax.optimization_barrier((jnp.concatenate([tail_m, prev_m]), own_o))
    older_o = swap(older_m)

    wide = jnp.transpose(queries.reshape(tokens, teams, HEADS * HD), (1, 0, 2))
    wide, _ = lax.optimization_barrier((wide, own_m))
    local = lax.all_to_all(wide, ("x", "y", "core"), 0, 0, tiled=True).reshape(plane, HEADS * HD)

    items, info, starts = plans(doc_ids, lax.axis_index("z") * plane, lax.axis_index("core"))
    out = attend(items, info, local, starts, (own_m, own_o, prev_m, tail_m, older_o))
    back = lax.all_to_all(out.reshape(teams, tokens, HEADS * HD), ("x", "y", "core"), 0, 0, tiled=True)
    return jnp.transpose(back, (1, 0, 2)).reshape(tokens, teams * HEADS * HD)


def solution(mesh):
    sizes = (16, 4, 4, 2)
    grid = Mesh(mesh.devices.reshape(sizes), AXES)

    def run(*args):
        return body(sizes, *args)

    return jax.shard_map(
        run,
        mesh=grid,
        in_specs=(P(AXES, None), P(AXES, None), P(AXES, None), P()),
        out_specs=P(AXES, None),
        check_vma=False,
    )
```

```python
import math

import jax
import jax.numpy as jnp
from jax import lax
from jax.experimental import pallas as pl
from jax.experimental.pallas import tpu as pltpu
from jax.sharding import Mesh
from jax.sharding import PartitionSpec as P

HD = 128
GRAN = 256
BACK = 10
OWN = 8
SPAN = 2
PAD = SPAN - 1
HALF = GRAN // 2
CHUNK = 64
HEADS = 2
COLS = HEADS * GRAN
ONES = 16
AXES = ("z", "x", "y", "core")
FACTOR = math.log2(math.e) / math.sqrt(HD)
HIDDEN = -2.0e30
FAR = 1 << 20
VMEM = pltpu.VMEM


def work(items, info, starts_ref, ks, vt, qt, spot, acc, peak, sa, sb):
    def scored(number, buffer):
        tile, first = items[0, number], items[1, number]
        keys = ks[pl.ds(first, SPAN)].reshape(SPAN * GRAN, 2 * HD)
        raw = jnp.dot(keys, qt[tile], preferred_element_type=jnp.float32)
        low = starts_ref[tile] - (first - PAD) * GRAN + items[2, number]
        place = jnp.concatenate([spot[...]] * (COLS // HD), axis=1)
        best = None
        for k in range(SPAN):
            rows = slice(k * GRAN, (k + 1) * GRAN)
            seen = place >= jnp.concatenate([low - k * GRAN] * HEADS, axis=1)
            if k == SPAN - 1:
                own = (BACK + tile - first) * GRAN + lax.broadcasted_iota(jnp.int32, (1, GRAN), 1)
                seen = seen & (place <= jnp.concatenate([own] * HEADS, axis=1))
            piece = jnp.where(seen, raw[rows], HIDDEN)
            buffer[rows] = piece
            most = jnp.max(piece.reshape(GRAN // 8, 8, COLS), axis=0)
            best = most if best is None else jnp.maximum(best, most)
        return jnp.max(best, axis=0, keepdims=True)

    def finish(number, buffer, best):
        tile, first = items[0, number], items[1, number]
        before = peak[tile]
        top = jnp.maximum(before, best)
        peak[tile] = top
        weights = jnp.exp2(buffer[...] - top).astype(jnp.bfloat16)
        values = vt[:, pl.ds(pl.multiple_of(first * GRAN, GRAN), SPAN * GRAN)]
        mixed = jnp.dot(values, weights, preferred_element_type=jnp.float32)
        acc[tile] = acc[tile] * jnp.exp2(before - top) + mixed

    def both(first, best):
        following = scored(first + 1, sb)
        finish(first, sa, best)
        best = scored(first + 2, sa)
        finish(first + 1, sb, following)
        return best

    def several(pairs, done, best):
        def group(number, best):
            for pair in range(pairs):
                best = both(2 * (done + pairs * number + pair), best)
            return best

        groups = lax.div(info[0] - done, pairs)
        return done + pairs * groups, lax.fori_loop(0, groups, group, best)

    done, best = 0, scored(0, sa)
    for pairs in (4, 2, 1):
        done, best = several(pairs, done, best)


def fill(info, groups, ks, vt, stage, spot, sems):
    copies = []
    for first, count, pair in groups:
        for half, source in enumerate(pair):
            rows = pl.ds(half * HALF, HALF)
            for part, there in (
                (0, ks.at[pl.ds(PAD + first, count), rows, pl.ds(0, HD)]),
                (0, ks.at[pl.ds(PAD + first, count), rows, pl.ds(HD, HD)]),
                (1, stage.at[pl.ds(first, count), rows, :]),
            ):
                copy = pltpu.make_async_copy(
                    source.at[:, :, pl.ds(part * HD, HD)], there, sems.at[len(copies)]
                )
                copy.start()
                copies.append(copy)
    granules = stage.shape[0]
    ks[:PAD] = jnp.zeros((PAD, GRAN, 2 * HD), jnp.bfloat16)
    vt[:, :PAD * GRAN] = jnp.zeros((HD + ONES, PAD * GRAN), jnp.bfloat16)
    vt[HD:, PAD * GRAN:] = jnp.ones((ONES, granules * GRAN), jnp.bfloat16)
    row = lax.broadcasted_iota(jnp.int32, (GRAN, HD), 0)
    holder = jnp.where(info[1] == 0, row // HALF, 1 - row // HALF)
    inner = row % HALF
    spot[...] = (inner // CHUNK) * (2 * CHUNK) + holder * CHUNK + inner % CHUNK
    return copies


def turn(granules, vt, stage):
    for g in range(granules):
        vt[:HD, (PAD + g) * GRAN:(PAD + g + 1) * GRAN] = stage[g].T


def kernel(
    items, info, q_ref, starts_ref, own_m, own_o, prev_m, prev_o, tail_m, tail_o,
    o_ref, qt, acc, peak, ks, vt, stage, spot, sa, sb, sems,
):
    tail = BACK - OWN
    groups = (BACK, OWN, (own_m, own_o)), (tail, OWN, (prev_m, prev_o)), (0, tail, (tail_m, tail_o))
    copies = fill(info, groups, ks, vt, stage, spot, sems)
    acc[...] = jnp.zeros_like(acc)
    peak[...] = jnp.full_like(peak, HIDDEN)
    for tile in range(OWN):
        for head in range(HEADS):
            cols = slice(head * GRAN, (head + 1) * GRAN)
            query = q_ref[tile * GRAN:(tile + 1) * GRAN, head * HD:(head + 1) * HD].T.astype(jnp.float32) * FACTOR
            coarse = query.astype(jnp.bfloat16)
            qt[tile, :HD, cols] = coarse
            qt[tile, HD:, cols] = (query - coarse.astype(jnp.float32)).astype(jnp.bfloat16)
    for copy in copies:
        copy.wait()
    turn(BACK + OWN, vt, stage)
    work(items, info, starts_ref, ks, vt, qt, spot, acc, peak, sa, sb)
    for tile in range(OWN):
        for head in range(HEADS):
            cols = slice(head * GRAN, (head + 1) * GRAN)
            o_ref[tile * GRAN:(tile + 1) * GRAN, head * HD:(head + 1) * HD] = (
                (acc[tile, :HD, cols] / acc[tile, HD:HD + 1, cols]).T.astype(jnp.bfloat16)
            )


LIMIT = pltpu.CompilerParams(vmem_limit_bytes=40 * 1024 * 1024)
INSIDE = pl.BlockSpec(memory_space=VMEM)
ANYWHERE = pl.BlockSpec(memory_space=pl.ANY)


def attend(items, info, queries, starts, pieces):
    window = BACK + OWN
    return pl.pallas_call(
        kernel,
        grid_spec=pltpu.PrefetchScalarGridSpec(
            num_scalar_prefetch=2,
            grid=(),
            in_specs=[INSIDE] * 2 + [ANYWHERE] * 6,
            out_specs=INSIDE,
            scratch_shapes=[
                VMEM((OWN, 2 * HD, COLS), jnp.bfloat16),
                VMEM((OWN, HD + ONES, COLS), jnp.float32),
                VMEM((OWN, 1, COLS), jnp.float32),
                VMEM((PAD + window, GRAN, 2 * HD), jnp.bfloat16),
                VMEM((HD + ONES, (PAD + window) * GRAN), jnp.bfloat16),
                VMEM((window, GRAN, HD), jnp.bfloat16),
                VMEM((GRAN, HD), jnp.int32),
                VMEM((SPAN * GRAN, COLS), jnp.float32),
                VMEM((SPAN * GRAN, COLS), jnp.float32),
                pltpu.SemaphoreType.DMA((18,)),
            ],
        ),
        out_shape=jax.ShapeDtypeStruct((OWN * GRAN, HEADS * HD), jnp.bfloat16),
        compiler_params=LIMIT,
        cost_estimate=pl.CostEstimate(flops=10**10, bytes_accessed=8 << 20, transcendentals=0),
    )(items, info, queries, starts, *pieces)


def pack_kernel(k_ref, v_ref, o_ref):
    copies = o_ref.shape[0] * HD // k_ref.shape[1]
    for place in range(o_ref.shape[0]):
        cols = slice(place // copies * HD, (place // copies + 1) * HD)
        o_ref[place, :, :HD] = k_ref[:, cols]
        o_ref[place, :, HD:] = v_ref[:, cols]


def pack(keys, values, chips):
    return pl.pallas_call(
        pack_kernel,
        in_specs=[INSIDE] * 2,
        out_specs=INSIDE,
        out_shape=jax.ShapeDtypeStruct((chips, keys.shape[0], 2 * HD), jnp.bfloat16),
    )(keys, values)


def agenda(counts, tops, room, core):
    tiles = jnp.arange(OWN, dtype=jnp.int32)
    ends = jnp.sum(jnp.where(tiles[None, :] <= tiles[:, None], counts[None, :], 0), axis=1)
    number = jnp.arange(room, dtype=jnp.int32)
    tile = jnp.minimum(jnp.sum(number[:, None] >= ends[None, :], axis=1, dtype=jnp.int32), OWN - 1)
    real = number < ends[-1]
    chosen = tile[:, None] == tiles[None, :]
    begin = jnp.sum(jnp.where(chosen, (ends - counts)[None, :], 0), axis=1)
    top = jnp.sum(jnp.where(chosen, tops[None, :], 0), axis=1)
    first = top - SPAN * jnp.where(real, number - begin, 0)
    items = jnp.stack([tile, first, jnp.where(real, 0, FAR)])
    return items, jnp.stack([(ends[-1] + 1) // 2, core])


def plans(doc_ids, first, core):
    plane = OWN * GRAN
    padded = jnp.concatenate([jnp.full((BACK * GRAN,), -1, jnp.int32), doc_ids])
    window = lax.dynamic_slice_in_dim(padded, first, (BACK + OWN) * GRAN, 0)
    ids = window[BACK * GRAN:]
    starts = jnp.sum(window[None, :] < ids[:, None], axis=1, dtype=jnp.int32)
    lows = starts[::GRAN] // GRAN
    tiles = jnp.arange(OWN, dtype=jnp.int32)
    items, info = agenda((BACK + tiles - lows) // SPAN + 1, BACK + tiles, 52, core)
    return items, info, starts.reshape(OWN, 1, GRAN)


def moved(value, sizes, there):
    zs, xs, ys, cores = sizes
    pairs = []
    for z in range(zs):
        for x in range(xs):
            for y in range(ys):
                for core in range(cores):
                    place = there(z, x, y, core)
                    if place is not None:
                        index = [((p[0] * xs + p[1]) * ys + p[2]) * cores + p[3] for p in ((z, x, y, core), place)]
                        pairs.append(tuple(index))
    return lax.ppermute(value, AXES, pairs)


def body(sizes, queries, keys, values, doc_ids):
    zs, xs, ys, cores = sizes
    chips = xs * ys
    teams = chips * cores
    tokens = queries.shape[0]
    plane = OWN * GRAN

    def swap(value):
        return moved(value, sizes, lambda z, x, y, core: (z, x, y, 1 - core))

    def later(value, planes):
        return moved(value, sizes, lambda z, x, y, core: (z + planes, x, y, core) if z + planes < zs else None)

    own_m = lax.all_to_all(pack(keys, values, chips), ("x", "y"), 0, 0, tiled=True).reshape(OWN, HALF, 2 * HD)
    prev_m = later(own_m, 1)
    tail_m = later(own_m[2 * OWN - BACK:], 2)
    prev_m, tail_m = lax.optimization_barrier((prev_m, tail_m))
    own_o = swap(own_m)
    prev_o = swap(prev_m)
    tail_o = swap(tail_m)

    wide = jnp.transpose(queries.reshape(tokens, teams, HEADS * HD), (1, 0, 2))
    wide, _ = lax.optimization_barrier((wide, own_m))
    local = lax.all_to_all(wide, ("x", "y", "core"), 0, 0, tiled=True).reshape(plane, HEADS * HD)

    items, info, starts = plans(doc_ids, lax.axis_index("z") * plane, lax.axis_index("core"))
    out = attend(items, info, local, starts, (own_m, own_o, prev_m, prev_o, tail_m, tail_o))
    back = lax.all_to_all(out.reshape(teams, tokens, HEADS * HD), ("x", "y", "core"), 0, 0, tiled=True)
    return jnp.transpose(back, (1, 0, 2)).reshape(tokens, teams * HEADS * HD)


def solution(mesh):
    sizes = (16, 4, 4, 2)
    grid = Mesh(mesh.devices.reshape(sizes), AXES)

    def run(*args):
        return body(sizes, *args)

    return jax.shard_map(
        run,
        mesh=grid,
        in_specs=(P(AXES, None), P(AXES, None), P(AXES, None), P()),
        out_specs=P(AXES, None),
        check_vma=False,
    )
```
